32 devices in a mesh: groups: 1, seq: 32 (over z, y, x, core).
Axes of the slice: x: 2, y: 2, z: 4, core: 2. Of those that a mesh axis runs over, the one named last changes fastest.
Arguments:
- token_ids: int32 [65536], P(('groups', 'seq')), may hold values from 0 to 30521
- embed_table: bfloat16 [1024, 30522], P('seq'), may hold values from -6 to 6
- right_blocks: bfloat16 [256, 256, 256], P('seq'), may hold values from -0.5 to 0.5
- right_pattern: int32 [256, 2, 2], P('seq'), may hold values 0 or 1
- left_blocks: bfloat16 [256, 256, 256], P('seq'), may hold values from -0.5 to 0.5
- left_pattern: int32 [256, 2, 2], P('seq'), may hold values 0 or 1
- value_gain: float32 [1024], replicated, may hold values from 0.1 to 1.9
- gate_gain: float32 [1024], replicated, may hold values from 0.1 to 1.9
- cotangent: bfloat16 [65536, 1024], P(('groups', 'seq')), may hold values from -0.375 to 0.375
Outputs:
- grad_right: bfloat16 [256, 256, 256], P(('groups', 'seq'))
- grad_left: bfloat16 [256, 256, 256], P(('groups', 'seq'))
- grad_value_gain: float32 [1024], P('groups')
- grad_gate_gain: float32 [1024], P('groups')
The draws below stay inside these ranges and needn't reach their ends.
Inputs may be any that keep to these rules, and one draw needn't show every extreme that they name: `right_pattern`: entry (b, r, s) is 1 where tile (r, s) of block b may be nonzero. `left_pattern`: entry (b, r, s) is 1 where tile (r, s) of block b may be nonzero.
All inputs are finite; a program needn't handle non-finite values.
Results may differ from the reference program's by a relative error of at most 0.0065.
Values may be sent and summed in bfloat16 or wider, within the bound.
A program may use at most 128 MiB of HBM per device.

```python
import math
import jax
import jax.numpy as jnp
import numpy as np
from jax import lax

G = 256
D = 1024
V = 30522
TILE = 128
NT = 2
L = 65536


def place_ends(values, key, least, high):
    place = [jax.random.randint(jax.random.fold_in(key, axis), (), 0, length) for axis, length in enumerate(values.shape)]
    longest = values.shape.index(max(values.shape))
    neighbour = place[:longest] + [(place[longest] + 1) % values.shape[longest]] + place[longest + 1:]
    return values.at[tuple(place)].set(least).at[tuple(neighbour)].set(high)


def block_levels(key, shape, cuts, least, largest):
    factor_of = 1.0
    for axis_at, shards_of in cuts:
        heights = jax.random.uniform(jax.random.fold_in(jax.random.fold_in(key, 6), axis_at), (shards_of,), jnp.float32, least / len(cuts), largest / len(cuts))
        factor_of = factor_of * jnp.repeat(jnp.exp(heights), shape[axis_at] // shards_of).reshape((-1,) + (1,) * (len(shape) - 1 - axis_at))
    return factor_of


def rank_table(amount, skew):
    weights = [(1 << 20) // math.isqrt(grade ** skew) + 1 for grade in range(1, amount + 1)]
    scale = 1 + sum(weights) // (1 << 30)
    return np.cumsum(np.array([max(1, weight // scale) for weight in weights]))


def ranked(rng, shape, count, skew):
    listing = rank_table(count, skew)
    pick = jax.random.randint(jax.random.fold_in(rng, 1), shape, 0, int(listing[count - 1]))
    standing = jnp.searchsorted(jnp.asarray(listing, jnp.int32), pick, side="right")
    return jax.random.permutation(jax.random.fold_in(rng, 2), count)[standing].astype(jnp.int32)


def centred(stream_key, extent, deviation, bound, shards=(), dtype=jnp.bfloat16):
    drawn = jax.random.normal(stream_key, extent, jnp.float32) * deviation
    if len(shards) > 0:
        drawn = block_levels(stream_key, extent, shards, -0.22, 0.18) * drawn
    return jnp.clip(drawn, min=-bound, max=bound).astype(dtype)


def setup_inputs(seed: int = 0, part: int = 0) -> dict:
    key_list = jax.random.split(jax.random.key(seed), 10)
    part_splits = jax.random.split(jax.random.fold_in(key_list[9], part), 10)
    token_ids = place_ends(ranked(part_splits[0], (L,), V, 1), jax.random.fold_in(part_splits[0], 3), 0, V - 1).astype(jnp.int32)
    embed_table = centred(key_list[1], (D, V), 1.0, 6.0, ((0, 32),))
    right_blocks = centred(key_list[2], (G, G, G), (G // 2) ** -0.5, 0.5, ((0, 32),))
    right_pattern = place_ends((jax.random.randint(key_list[3], (G, NT, NT), 0, 2) < 1).astype(jnp.int32), jax.random.fold_in(key_list[3], 1), 0, 1)
    left_blocks = centred(key_list[4], (G, G, G), (G // 2) ** -0.5, 0.5, ((0, 32),))
    left_pattern = place_ends((jax.random.randint(key_list[5], (G, NT, NT), 0, 2) < 1).astype(jnp.int32), jax.random.fold_in(key_list[5], 1), 0, 1)
    value_gain = jnp.clip(1.0 + 0.18 * jax.random.normal(key_list[6], (D,), jnp.float32), 0.1, 1.9)
    gate_gain = jnp.clip(1.0 + 0.18 * jax.random.normal(key_list[7], (D,), jnp.float32), 0.1, 1.9)
    cotangent = centred(part_splits[8], (L, D), 0.0625, 0.375, ((0, 32),))
    return {"token_ids": token_ids, "embed_table": embed_table, "right_blocks": right_blocks, "right_pattern": right_pattern, "left_blocks": left_blocks, "left_pattern": left_pattern, "value_gain": value_gain, "gate_gain": gate_gain, "cotangent": cotangent}


def expand_pattern(pattern):
    return jnp.repeat(jnp.repeat(pattern, TILE, axis=0), TILE, axis=1).astype(jnp.bfloat16)


def reference(token_ids, embed_table, right_blocks, right_pattern, left_blocks, left_pattern, value_gain, gate_gain, cotangent):
    x_grid = jnp.take(embed_table, token_ids, axis=1).T.reshape(G, G, D)
    values = (x_grid.astype(jnp.float32) * value_gain).astype(jnp.bfloat16)

    def right_forward(operands):
        block, pattern, value_rows = operands
        return jnp.dot(block * expand_pattern(pattern), value_rows, preferred_element_type=jnp.float32).astype(jnp.bfloat16)

    row_mixed = lax.map(right_forward, (right_blocks, right_pattern, values))
    column_view = jnp.transpose(row_mixed, (1, 0, 2))

    def left_forward(operands):
        block, pattern, column = operands
        return jnp.dot(block * expand_pattern(pattern), column, preferred_element_type=jnp.float32).astype(jnp.bfloat16)

    mixed_cols = lax.map(left_forward, (left_blocks, left_pattern, column_view))
    mixed = jnp.transpose(mixed_cols, (1, 0, 2))
    inputs_f32 = x_grid.astype(jnp.float32)
    gate_value = jax.nn.sigmoid(inputs_f32 * gate_gain)
    grad_out = cotangent.reshape(G, G, D).astype(jnp.float32)
    grad_gate_gain = jnp.sum(grad_out * mixed.astype(jnp.float32) * gate_value * (1.0 - gate_value) * inputs_f32, axis=(0, 1))
    grad_mixed = (grad_out * gate_value).astype(jnp.bfloat16)
    grad_mixed_cols = jnp.transpose(grad_mixed, (1, 0, 2))

    def left_backward(operands):
        block, pattern, grad_column, column = operands
        pattern_full = expand_pattern(pattern)
        grad_rows = jnp.dot((block * pattern_full).T, grad_column, preferred_element_type=jnp.float32).astype(jnp.bfloat16)
        grad_block = (jnp.dot(grad_column, column.T, preferred_element_type=jnp.float32) * pattern_full.astype(jnp.float32)).astype(jnp.bfloat16)
        return grad_rows, grad_block

    grad_row_cols, grad_left = lax.map(left_backward, (left_blocks, left_pattern, grad_mixed_cols, column_view))
    grad_row_mixed = jnp.transpose(grad_row_cols, (1, 0, 2))

    def right_backward(operands):
        block, pattern, grad_rows, value_rows, input_rows = operands
        pattern_full = expand_pattern(pattern)
        grad_values = jnp.dot((block * pattern_full).T, grad_rows, preferred_element_type=jnp.float32)
        grad_block = (jnp.dot(grad_rows, value_rows.T, preferred_element_type=jnp.float32) * pattern_full.astype(jnp.float32)).astype(jnp.bfloat16)
        return grad_block, jnp.sum(grad_values * input_rows.astype(jnp.float32), axis=0)

    grad_right, gain_terms = lax.map(right_backward, (right_blocks, right_pattern, grad_row_mixed, values, x_grid))
    grad_value_gain = jnp.sum(gain_terms, axis=0)
    return grad_right, grad_left, grad_value_gain, grad_gate_gain
```

```python
import jax
import jax.numpy as jnp
from jax import lax
from jax.sharding import PartitionSpec as P


def expand_pattern(pattern, tile_size):
    return jnp.repeat(jnp.repeat(pattern, tile_size, axis=1), tile_size, axis=2).astype(
        jnp.bfloat16
    )


def make_local(devices):
    splits = 4 if devices % 4 == 0 else 1
    plane = devices // splits
    plane_groups = [[s * plane + p for p in range(plane)] for s in range(splits)]
    split_groups = [[s * plane + p for s in range(splits)] for p in range(plane)]

    def local(
        token_ids,
        embed_table,
        right_blocks,
        right_pattern,
        left_blocks,
        left_pattern,
        value_gain,
        gate_gain,
        cotangent,
    ):
        rows = right_blocks.shape[0]
        side = right_blocks.shape[1]
        channels = value_gain.shape[0]
        part = channels // splits
        held = splits * rows
        tile_size = side // right_pattern.shape[1]
        me = lax.axis_index("seq")
        my_split, my_place = me // plane, me % plane

        every_id = lax.all_gather(token_ids, "seq", axis=0, tiled=True)
        table = lax.all_gather(
            embed_table, "seq", axis=0, tiled=True, axis_index_groups=plane_groups
        )
        right_mask = expand_pattern(right_pattern, tile_size)
        left_mask = expand_pattern(left_pattern, tile_size)
        right_eff = lax.all_gather(
            right_blocks * right_mask, "seq", axis=0, tiled=True, axis_index_groups=split_groups
        )
        left_eff = lax.all_gather(
            left_blocks * left_mask, "seq", axis=0, tiled=True, axis_index_groups=split_groups
        )
        sent = cotangent.reshape(rows, splits, plane, rows, splits, part)
        sent = sent.transpose(4, 2, 1, 3, 0, 5).reshape(devices, held, rows, part)
        came = lax.all_to_all(sent, "seq", split_axis=0, concat_axis=0, tiled=True)
        grad_out = came.transpose(1, 0, 2, 3).reshape(held, side, part)

        row_ids = lax.dynamic_index_in_dim(
            every_id.reshape(splits, plane, rows, side), my_place, 1, keepdims=False
        ).reshape(-1)
        column_ids = (
            lax.dynamic_index_in_dim(
                every_id.reshape(side, splits, plane, rows), my_place, 2, keepdims=False
            )
            .reshape(side, held)
            .T.reshape(-1)
        )
        looked_up = jnp.take(table.T, jnp.concatenate([row_ids, column_ids]), axis=0, mode="clip")
        looked_up = looked_up.reshape(2, held, side, part)
        x_rows, x_columns = looked_up[0], looked_up[1]
        my_value_gain = lax.dynamic_slice_in_dim(value_gain, my_split * part, part)
        my_gate_gain = lax.dynamic_slice_in_dim(gate_gain, my_split * part, part)

        values = (x_rows.astype(jnp.float32) * my_value_gain).astype(jnp.bfloat16)
        row_mixed = jnp.einsum(
            "ikj,ijc->ikc", right_eff, values, preferred_element_type=jnp.float32
        ).astype(jnp.bfloat16)
        sent = row_mixed.reshape(splits, rows, splits, plane, rows, part)
        sent = sent.transpose(3, 2, 4, 0, 1, 5).reshape(plane, held, splits, rows, part)
        came = lax.all_to_all(
            sent, "seq", split_axis=0, concat_axis=0, tiled=True, axis_index_groups=plane_groups
        )
        column_view = came.transpose(1, 2, 0, 3, 4).reshape(held, side, part)

        mixed = jnp.einsum(
            "kai,kic->kac", left_eff, column_view, preferred_element_type=jnp.float32
        )
        inputs_f32 = x_columns.astype(jnp.float32)
        gate_value = jax.nn.sigmoid(inputs_f32 * my_gate_gain)
        gated = grad_out.astype(jnp.float32) * gate_value
        grad_mixed = gated.astype(jnp.bfloat16)
        product = gated * mixed
        value_term = jnp.sum(product, axis=(0, 1)) / my_value_gain
        gate_term = jnp.sum(product * (1.0 - gate_value) * inputs_f32, axis=(0, 1))

        grad_rows = jnp.einsum(
            "kai,kac->kic", left_eff, grad_mixed, preferred_element_type=jnp.float32
        ).astype(jnp.bfloat16)
        sent = grad_rows.reshape(held, splits, plane, rows, part).transpose(2, 0, 1, 3, 4)
        came = lax.all_to_all(
            sent, "seq", split_axis=0, concat_axis=0, tiled=True, axis_index_groups=plane_groups
        )
        grad_row_mixed = (
            came.reshape(plane, splits, rows, held, part)
            .transpose(3, 1, 0, 2, 4)
            .reshape(held, side, part)
        )
        left_part = jnp.einsum(
            "kac,kic->kai", grad_mixed, column_view, preferred_element_type=jnp.float32
        ).astype(jnp.bfloat16)

        def gathered_sum(terms, mask):
            came = lax.all_to_all(
                terms.reshape(splits, rows, side, side),
                "seq",
                split_axis=0,
                concat_axis=0,
                tiled=True,
                axis_index_groups=split_groups,
            )
            total = jnp.sum(came.astype(jnp.float32), axis=0)
            return (total * mask.astype(jnp.float32)).astype(jnp.bfloat16)

        grad_left = gathered_sum(left_part, left_mask)
        right_part = jnp.einsum(
            "ikc,ijc->ikj", grad_row_mixed, values, preferred_element_type=jnp.float32
        ).astype(jnp.bfloat16)
        grad_right = gathered_sum(right_part, right_mask)

        blank = jnp.zeros((2, channels), jnp.float32)
        terms = lax.dynamic_update_slice(
            blank, jnp.stack([value_term, gate_term]), (0, my_split * part)
        )
        totals = lax.psum(terms, "seq")
        return grad_right, grad_left, totals[0], totals[1]

    return local


def solution(mesh):
    return jax.shard_map(
        make_local(mesh.shape["seq"]),
        mesh=mesh,
        in_specs=(
            P(("groups", "seq")),
            P("seq", None),
            P("seq", None, None),
            P("seq", None, None),
            P("seq", None, None),
            P("seq", None, None),
            P(),
            P(),
            P(("groups", "seq"), None),
        ),
        out_specs=(
            P(("groups", "seq"), None, None),
            P(("groups", "seq"), None, None),
            P("groups"),
            P("groups"),
        ),
        check_vma=False,
    )
```
